32 devices in a mesh: parts: 2 (over y), layer: 2 (over core), row: 2 (over x), col: 4 (over z).
Axes of the slice: x: 2, y: 2, z: 4, core: 2. Of those that a mesh axis runs over, the one named last changes fastest.
Arguments:
- density_blocks: bfloat16 [192, 256, 64], P(('parts', 'layer', 'row'), 'col'), parts along dimension 0, may hold values from -0.5 to 0.5
- left_index: int32 [192, 16, 8], P(('parts', 'row'), 'col'), parts along dimension 0, may hold values from 0 to 23
- right_index: int32 [192, 16, 8], P(('parts', 'row'), 'col'), parts along dimension 0, may hold values from 0 to 23
- pair_count: int32 [192, 16], P(('parts', 'row'), 'col'), parts along dimension 0, may hold values from 1 to 8, as said below
Outputs:
- square: bfloat16 [192, 256, 64], P(('parts', 'layer', 'row'), 'col'), parts along dimension 0
The draws below stay inside these ranges and needn't reach their ends.
There are 2 independent parts, one for each index of `parts`. The reference program is written for one: setup_inputs(seed, part) draws one part's arguments, and reference() takes and returns one part's arrays. A program takes and returns all parts, laid end to end along the dimension named above; each array names one. Nothing has to cross between parts.
Inputs may be any that keep to these rules, and one draw needn't show every extreme that they name: `pair_count`: every result panel has at least one result block and inner panel with 8 live pairs; the same pair may be listed twice and then counts twice.
All inputs are finite; a program needn't handle non-finite values.
Results may differ from the reference program's by a relative error of at most 0.001.
Values may be sent and summed in bfloat16 or wider, within the bound.
A program may use at most 64 MiB of HBM per device.

```python
import jax
import jax.numpy as jnp
from jax import lax

BLK = 64
NS = 24
KP = 8
GRID = 4
N_LAYER = 2
N_ROW = 2
N_COL = 4


def draw_pair_count(key, part):
    key = jax.random.fold_in(key, 7)
    key_level, key_base, key_slot, key_inner = jax.random.split(key, 4)
    panel_shape = (N_ROW, N_LAYER, 1, N_COL, 1)
    busy_level = jax.random.randint(key_level, panel_shape, max(1, KP // 4), KP + 1)
    base_draw = jax.random.randint(key_base, (N_ROW, N_LAYER, NS, N_COL, GRID), 0, 4096)
    counts = 1 + base_draw % busy_level
    slot_pick = jax.random.randint(key_slot, panel_shape, 0, NS)
    inner_pick = jax.random.randint(key_inner, panel_shape, 0, GRID)
    slot_iota = lax.broadcasted_iota(jnp.int32, (1, 1, NS, 1, 1), 2)
    inner_iota = lax.broadcasted_iota(jnp.int32, (1, 1, 1, 1, GRID), 4)
    forced = (slot_iota == slot_pick) & (inner_iota == inner_pick)
    counts = jnp.where(forced, KP, counts)
    return counts.reshape(N_ROW * N_LAYER * NS, N_COL * GRID).astype(jnp.int32)


def set_ends(entries, own_key, least, largest):
    longest = entries.shape.index(max(entries.shape))
    spots = []
    for shift in (0, 1):
        where = [jax.random.randint(jax.random.fold_in(own_key, axis), (), 0, length) for axis, length in enumerate(entries.shape)]
        where[longest] = (where[longest] + shift) % entries.shape[longest]
        spots.append(tuple(where))
    return entries.at[spots[0]].set(least).at[spots[1]].set(largest)


def levels(rng, dims, cuts, least, high):
    gain = 1.0
    for position, parts in cuts:
        steps = jax.random.uniform(jax.random.fold_in(jax.random.fold_in(rng, 6), position), (parts,), jnp.float32, least / len(cuts), high / len(cuts))
        gain = gain * jnp.repeat(jnp.exp(steps), dims[position] // parts).reshape((-1,) + (1,) * (len(dims) - 1 - position))
    return gain


def bell_draw(own_key, extent, spread, bound, shards=(), kind=jnp.bfloat16):
    values = spread * jax.random.normal(own_key, extent, jnp.float32)
    if shards:
        values = values * levels(own_key, extent, shards, -0.22, 0.18)
    return jnp.clip(values, -bound, bound).astype(kind)


def setup_inputs(seed: int = 0, part: int = 0) -> dict:
    streams_of = jax.random.split(jax.random.key(seed), 5)
    own_keys = jax.random.split(jax.random.fold_in(streams_of[4], part), 5)
    return {
        "density_blocks": bell_draw(own_keys[0], (GRID * NS, N_COL * BLK, BLK), (2 * BLK) ** -0.5, 0.5, ((0, 4), (1, 4))),
        "left_index": set_ends(jax.random.randint(own_keys[1], (N_ROW * N_LAYER * NS, N_COL * GRID, KP), 0, NS), jax.random.fold_in(own_keys[1], 1), 0, NS - 1).astype(jnp.int32),
        "right_index": set_ends(jax.random.randint(own_keys[2], (N_ROW * N_LAYER * NS, N_COL * GRID, KP), 0, NS), jax.random.fold_in(own_keys[2], 1), 0, NS - 1).astype(jnp.int32),
        "pair_count": draw_pair_count(jax.random.fold_in(jax.random.fold_in(streams_of[4], part), 71), part),
    }


def reference(density_blocks, left_index, right_index, pair_count):
    panels = density_blocks.reshape(GRID, NS, N_COL, BLK, BLK)
    lists_left = left_index.reshape(N_ROW, N_LAYER, NS, N_COL, GRID, KP)
    lists_right = right_index.reshape(N_ROW, N_LAYER, NS, N_COL, GRID, KP)
    lists_count = pair_count.reshape(N_ROW, N_LAYER, NS, N_COL, GRID)
    inner_iota = jnp.arange(GRID, dtype=jnp.int32)
    pair_iota = jnp.arange(KP, dtype=jnp.int32)

    def one_panel(flat_index):
        group_index = flat_index // N_COL
        column_index = flat_index % N_COL
        row_index = group_index % N_ROW
        layer_index = group_index // N_ROW
        left_panels = jnp.transpose(panels[group_index], (1, 0, 2, 3))
        right_panels = panels[:, :, column_index]
        chosen_left = lists_left[row_index, layer_index, :, column_index]
        chosen_right = lists_right[row_index, layer_index, :, column_index]
        counts = lists_count[row_index, layer_index, :, column_index]
        picked_left = left_panels[inner_iota[None, :, None], chosen_left].astype(jnp.float32)
        picked_right = right_panels[inner_iota[None, :, None], chosen_right].astype(jnp.float32)
        live_mask = pair_iota[None, None, :] < counts[:, :, None]
        picked_right = jnp.where(live_mask[..., None, None], picked_right, jnp.zeros((), picked_right.dtype))
        return jnp.einsum("okpij,okpjl->oil", picked_left, picked_right)

    result = lax.map(one_panel, jnp.arange(GRID * N_COL, dtype=jnp.int32))
    result = result.reshape(GRID, N_COL, NS, BLK, BLK).transpose(0, 2, 1, 3, 4)
    return result.reshape(GRID * NS, N_COL * BLK, BLK).astype(jnp.bfloat16)
```

```python
import functools

import jax
import jax.numpy as jnp
from jax import lax
from jax.experimental import pallas as pl
from jax.experimental.pallas import tpu as pltpu
from jax.sharding import PartitionSpec as P

MESH = pl.DeviceIdType.MESH


def kernel(
    cols, rows, layers, chunks,
    x_hbm, li_hbm, ri_hbm, cnt_hbm, out_ref,
    x_v, li_s, ri_s, cnt_s, lefts, rights, work_l, work_r, acc,
    in_sem, idx_sem, send_z, recv_z, send_x, recv_x,
):
    ns, blk, _ = x_hbm.shape
    half = ns // 2
    step_rows = half // chunks
    pairs = li_hbm.shape[2]
    c = lax.axis_index("col")
    layer = lax.axis_index("layer")
    row = lax.axis_index("row")
    r = layer * rows + row
    group = layers * rows

    own_rows = pl.ds(layer * ns, ns)
    x_copy = pltpu.make_async_copy(x_hbm, x_v, in_sem)
    x_copy.start()
    idx_copies = [
        pltpu.make_async_copy(src.at[own_rows], dst, idx_sem.at[j])
        for j, (src, dst) in enumerate(((li_hbm, li_s), (ri_hbm, ri_s), (cnt_hbm, cnt_s)))
    ]
    for copy in idx_copies:
        copy.start()

    barrier = pltpu.get_barrier_semaphore()

    @pl.when(c > 0)
    def _():
        pl.semaphore_signal(barrier, inc=1, device_id={"col": c - 1}, device_id_type=MESH)

    @pl.when(c < cols - 1)
    def _():
        pl.semaphore_signal(barrier, inc=1, device_id={"col": c + 1}, device_id_type=MESH)

    def mate(j):
        other = lax.rem(r + j, group)
        return other, {"layer": other // rows, "row": lax.rem(other, rows)}

    for j in range(1, group):
        pl.semaphore_signal(barrier, inc=1, device_id=mate(j)[1], device_id_type=MESH)

    x_copy.wait()
    for s in range(half):
        lefts[c, s] = jnp.concatenate([x_v[s], x_v[s + half]], axis=-1)
    near = jnp.where(c > 0, 1, 0) + jnp.where(c < cols - 1, 1, 0)
    pl.semaphore_wait(barrier, near + (group - 1))

    def z_copy(panel, chunk, way):
        part = lefts.at[panel, pl.ds(chunk * step_rows, step_rows)]
        return pltpu.make_async_remote_copy(
            src_ref=part,
            dst_ref=part,
            send_sem=send_z.at[way, panel, chunk],
            recv_sem=recv_z.at[panel, chunk],
            device_id={"col": c + (1 if way == 0 else -1)},
            device_id_type=MESH,
        )

    def x_copy_to(j):
        return pltpu.make_async_remote_copy(
            src_ref=lefts.at[c],
            dst_ref=rights.at[r],
            send_sem=send_x.at[j],
            recv_sem=recv_x.at[r],
            device_id=mate(j)[1],
            device_id_type=MESH,
        )

    def on_way(way, do):
        pl.when(c < cols - 1 if way == 0 else c > 0)(do)

    for chunk in range(chunks):
        for way in (0, 1):
            on_way(way, lambda chunk=chunk, way=way: z_copy(c, chunk, way).start())
        if chunk == 0:
            for j in range(1, group):
                x_copy_to(j).start()
    rights[r] = lefts[c]
    work_r[ns] = jnp.zeros_like(work_r[ns])
    acc[...] = jnp.zeros_like(acc)
    low = lax.broadcasted_iota(jnp.int32, (blk, 2 * blk), 1) < blk
    for copy in idx_copies:
        copy.wait()

    def multiply(k):
        @pl.when(k != r)
        def _():
            pltpu.make_async_remote_copy(
                src_ref=lefts.at[c],
                dst_ref=rights.at[k],
                send_sem=send_x.at[0],
                recv_sem=recv_x.at[k],
                device_id=mate(1)[1],
                device_id_type=MESH,
            ).wait_recv()

        for s in range(half):
            block = lefts[k, s]
            turned = jnp.concatenate([block[:, blk:], block[:, :blk]], axis=-1)
            work_l[s] = block
            work_l[s + half] = turned
            work_l[s + 2 * half] = block
            block = rights[k, s]
            work_r[s] = block
            work_r[s + half] = jnp.concatenate([block[:, blk:], block[:, :blk]], axis=-1)

        def one(o, carry):
            count = cnt_s[o, k]
            left, right = [], []
            for p in range(0, pairs, 2):
                first = work_l[li_s[o, k, p]]
                second = work_l[li_s[o, k, p + 1] + half]
                left.append(jnp.where(low, first, second))
                for q in (p, p + 1):
                    right.append(work_r[jnp.where(q < count, ri_s[o, k, q], ns)])
            acc[o] += jnp.dot(
                jnp.concatenate(left, axis=1),
                jnp.concatenate(right, axis=0),
                preferred_element_type=jnp.float32,
            )
            return carry

        lax.fori_loop(0, ns, one, 0, unroll=2)

    multiply(c)

    def step(s, carry):
        from_low = c - 1 - s
        from_high = c + 1 + s
        for chunk in range(chunks):

            @pl.when(from_low >= 0)
            def _(chunk=chunk):
                z_copy(from_low, chunk, 0).wait_recv()

                @pl.when(c < cols - 1)
                def _():
                    z_copy(from_low, chunk, 0).start()

            @pl.when(from_high < cols)
            def _(chunk=chunk):
                z_copy(from_high, chunk, 1).wait_recv()

                @pl.when(c > 0)
                def _():
                    z_copy(from_high, chunk, 1).start()

        @pl.when(from_low >= 0)
        def _():
            multiply(from_low)

        @pl.when(from_high < cols)
        def _():
            multiply(from_high)

        return carry

    lax.fori_loop(0, cols - 1, step, 0)

    for o in range(ns):
        out_ref[o] = acc[o][:, :blk].astype(out_ref.dtype)

    def drain(panel, carry):
        for chunk in range(chunks):

            @pl.when((c < cols - 1) & (panel <= c))
            def _(chunk=chunk):
                z_copy(panel, chunk, 0).wait_send()

            @pl.when((c > 0) & (panel >= c))
            def _(chunk=chunk):
                z_copy(panel, chunk, 1).wait_send()

        return carry

    lax.fori_loop(0, cols, drain, 0)
    for j in range(1, group):
        x_copy_to(j).wait_send()


def on_device(density_blocks, left_index, right_index, pair_count):
    ns, blk, _ = density_blocks.shape
    cols = lax.axis_size("col")
    rows = lax.axis_size("row")
    layers = lax.axis_size("layer")
    inner = left_index.shape[1]
    pairs = left_index.shape[2]
    half = ns // 2
    chunks = 2 if half % 2 == 0 else 1
    group = rows * layers
    packed = (half, blk, 2 * blk)
    return pl.pallas_call(
        functools.partial(kernel, cols, rows, layers, chunks),
        out_shape=jax.ShapeDtypeStruct((ns, blk, blk), jnp.bfloat16),
        in_specs=[pl.BlockSpec(memory_space=pl.ANY)] * 4,
        out_specs=pl.BlockSpec(memory_space=pltpu.VMEM),
        scratch_shapes=[
            pltpu.VMEM((ns, blk, blk), jnp.bfloat16),
            pltpu.SMEM((ns, inner, pairs), jnp.int32),
            pltpu.SMEM((ns, inner, pairs), jnp.int32),
            pltpu.SMEM((ns, inner), jnp.int32),
            pltpu.VMEM((cols,) + packed, jnp.bfloat16),
            pltpu.VMEM((group,) + packed, jnp.bfloat16),
            pltpu.VMEM((3 * half, blk, 2 * blk), jnp.bfloat16),
            pltpu.VMEM((ns + 1, blk, 2 * blk), jnp.bfloat16),
            pltpu.VMEM((ns, blk, 2 * blk), jnp.float32),
            pltpu.SemaphoreType.DMA,
            pltpu.SemaphoreType.DMA((3,)),
            pltpu.SemaphoreType.DMA((2, cols, chunks)),
            pltpu.SemaphoreType.DMA((cols, chunks)),
            pltpu.SemaphoreType.DMA((group,)),
            pltpu.SemaphoreType.DMA((group,)),
        ],
        compiler_params=pltpu.CompilerParams(
            collective_id=0, has_side_effects=True, vmem_limit_bytes=32 * 1024 * 1024
        ),
    )(density_blocks, left_index, right_index, pair_count)


def solution(mesh):
    placed = (
        P(("parts", "layer", "row"), "col", None),
        P(("parts", "row"), "col", None),
        P(("parts", "row"), "col", None),
        P(("parts", "row"), "col"),
    )
    return jax.shard_map(
        on_device,
        mesh=mesh,
        in_specs=placed,
        out_specs=P(("parts", "layer", "row"), "col", None),
        check_vma=False,
    )
```

```python
import functools

import jax
import jax.numpy as jnp
from jax import lax
from jax.experimental import pallas as pl
from jax.experimental.pallas import tpu as pltpu
from jax.sharding import PartitionSpec as P

UNROLL = 24
MESH = pl.DeviceIdType.MESH


def kernel(
    cols, rows, layers, chunks,
    x_hbm, li_hbm, ri_hbm, cnt_hbm, out_ref,
    x_v, li_s, ri_s, cnt_s, lefts, rights, work_l, work_r, acc,
    in_sem, idx_sem, send_z, recv_z, send_x, send_l, recv_x,
):
    ns, blk, _ = x_hbm.shape
    half = ns // 2
    step_rows = half // chunks
    pairs = li_hbm.shape[1]
    c = lax.axis_index("col")
    layer = lax.axis_index("layer")
    row = lax.axis_index("row")
    r = layer * rows + row

    x_copy = pltpu.make_async_copy(x_hbm, x_v, in_sem)
    x_copy.start()
    idx_copies = [
        pltpu.make_async_copy(src, dst, idx_sem.at[j])
        for j, (src, dst) in enumerate(((li_hbm, li_s), (ri_hbm, ri_s), (cnt_hbm, cnt_s)))
    ]
    for copy in idx_copies:
        copy.start()

    barrier = pltpu.get_barrier_semaphore()

    @pl.when(c > 0)
    def _():
        pl.semaphore_signal(barrier, inc=1, device_id={"col": c - 1}, device_id_type=MESH)

    @pl.when(c < cols - 1)
    def _():
        pl.semaphore_signal(barrier, inc=1, device_id={"col": c + 1}, device_id_type=MESH)

    def row_mate(j):
        other = lax.rem(row + j, rows)
        return other, {"row": other}

    def layer_mate(j):
        other = lax.rem(layer + j, layers)
        return other, {"layer": other}

    for j in range(1, rows):
        pl.semaphore_signal(barrier, inc=1, device_id=row_mate(j)[1], device_id_type=MESH)
    for j in range(1, layers):
        pl.semaphore_signal(barrier, inc=1, device_id=layer_mate(j)[1], device_id_type=MESH)

    x_copy.wait()
    for s in range(half):
        both = jnp.concatenate([x_v[s], x_v[s + half]], axis=-1)
        lefts[c, s] = both
        rights[r, s] = both
    near = jnp.where(c > 0, 1, 0) + jnp.where(c < cols - 1, 1, 0)
    pl.semaphore_wait(barrier, near + (rows - 1) + (layers - 1))

    def z_copy(panel, chunk, way):
        part = lefts.at[panel, pl.ds(chunk * step_rows, step_rows)]
        return pltpu.make_async_remote_copy(
            src_ref=part,
            dst_ref=part,
            send_sem=send_z.at[way, panel, chunk],
            recv_sem=recv_z.at[panel, chunk],
            device_id={"col": c + (1 if way == 0 else -1)},
            device_id_type=MESH,
        )

    def row_copy(j):
        return pltpu.make_async_remote_copy(
            src_ref=lefts.at[c],
            dst_ref=rights.at[r],
            send_sem=send_x.at[j],
            recv_sem=recv_x.at[r],
            device_id=row_mate(j)[1],
            device_id_type=MESH,
        )

    def layer_copy(j, other):
        panel = layer * rows + other
        return pltpu.make_async_remote_copy(
            src_ref=rights.at[panel],
            dst_ref=rights.at[panel],
            send_sem=send_l.at[j, other],
            recv_sem=recv_x.at[panel],
            device_id=layer_mate(j)[1],
            device_id_type=MESH,
        )

    def right_landed(panel):
        pltpu.make_async_remote_copy(
            src_ref=rights.at[panel],
            dst_ref=rights.at[panel],
            send_sem=send_x.at[0],
            recv_sem=recv_x.at[panel],
            device_id=row_mate(1)[1],
            device_id_type=MESH,
        ).wait_recv()

    def on_way(way, do):
        pl.when(c < cols - 1 if way == 0 else c > 0)(do)

    for chunk in range(chunks):
        for way in (0, 1):
            on_way(way, lambda chunk=chunk, way=way: z_copy(c, chunk, way).start())
        if chunk == 0:
            for j in range(1, rows):
                row_copy(j).start()
            for j in range(1, layers):
                layer_copy(j, row).start()
    work_r[ns] = jnp.zeros_like(work_r[ns])
    acc[...] = jnp.zeros_like(acc)
    low = lax.broadcasted_iota(jnp.int32, (blk, 2 * blk), 1) < blk
    for copy in idx_copies:
        copy.wait()

    def multiply(k):
        @pl.when(k // rows != layer)
        def _():
            right_landed(k)

        for s in range(half):
            block = lefts[k, s]
            turned = jnp.concatenate([block[:, blk:], block[:, :blk]], axis=-1)
            work_l[s] = block
            work_l[s + half] = turned
            work_l[s + 2 * half] = block
            block = rights[k, s]
            work_r[s] = block
            work_r[s + half] = jnp.concatenate([block[:, blk:], block[:, :blk]], axis=-1)

        def one(o, carry):
            at = layer * ns + o
            count = cnt_s[k, at]
            left, right = [], []
            for p in range(0, pairs, 2):
                first = work_l[li_s[k, p, at]]
                second = work_l[li_s[k, p + 1, at] + half]
                left.append(jnp.where(low, first, second))
                for q in (p, p + 1):
                    right.append(work_r[jnp.where(q < count, ri_s[k, q, at], ns)])
            acc[o] += jnp.dot(
                jnp.concatenate(left, axis=1),
                jnp.concatenate(right, axis=0),
                preferred_element_type=jnp.float32,
            )
            return carry

        lax.fori_loop(0, ns, one, 0, unroll=UNROLL)

    shorter = jnp.minimum(c, cols - 1 - c)
    longer = jnp.maximum(c, cols - 1 - c)

    def turn(i):
        both = i <= 2 * shorter
        distance = jnp.where(both, (i + 1) // 2, i - shorter)
        lower = jnp.where(both, lax.rem(i, 2) == 1, c == longer)
        return jnp.where(lower, c - distance, c + distance)

    def landed(distance):
        return 1 + jnp.minimum(c, distance) + jnp.minimum(cols - 1 - c, distance)

    def multiply_turn(i, carry):
        multiply(turn(i))
        return carry

    def step(s, done):
        from_low = c - 1 - s
        from_high = c + 1 + s
        for chunk in range(chunks):

            @pl.when(from_low >= 0)
            def _(chunk=chunk):
                z_copy(from_low, chunk, 0).wait_recv()

                @pl.when(c < cols - 1)
                def _():
                    z_copy(from_low, chunk, 0).start()

            @pl.when(from_high < cols)
            def _(chunk=chunk):
                z_copy(from_high, chunk, 1).wait_recv()

                @pl.when(c > 0)
                def _():
                    z_copy(from_high, chunk, 1).start()

        @pl.when(s == 0)
        def _():
            for j in range(1, rows):
                other = row_mate(j)[0]
                right_landed(layer * rows + other)
                for to in range(1, layers):
                    layer_copy(to, other).start()

        eager = (shorter == 0) | (s + 1 >= longer)
        until = jnp.where(eager, landed(s + 1), landed(s))
        lax.fori_loop(done, until, multiply_turn, 0)
        return until

    lax.fori_loop(0, cols - 1, step, 0)

    for o in range(ns):
        out_ref[o] = acc[o][:, :blk].astype(out_ref.dtype)

    def drain(panel, carry):
        for chunk in range(chunks):

            @pl.when((c < cols - 1) & (panel <= c))
            def _(chunk=chunk):
                z_copy(panel, chunk, 0).wait_send()

            @pl.when((c > 0) & (panel >= c))
            def _(chunk=chunk):
                z_copy(panel, chunk, 1).wait_send()

        return carry

    lax.fori_loop(0, cols, drain, 0)
    for j in range(1, rows):
        row_copy(j).wait_send()
    for j in range(1, layers):
        for other in range(rows):
            layer_copy(j, other).wait_send()


def on_device(density_blocks, left_index, right_index, pair_count):
    ns, blk, _ = density_blocks.shape
    cols = lax.axis_size("col")
    rows = lax.axis_size("row")
    layers = lax.axis_size("layer")
    left_index = jnp.transpose(left_index, (1, 2, 0))
    right_index = jnp.transpose(right_index, (1, 2, 0))
    pair_count = jnp.transpose(pair_count, (1, 0))
    half = ns // 2
    chunks = 3 if half % 3 == 0 else 1
    group = rows * layers
    packed = (half, blk, 2 * blk)
    return pl.pallas_call(
        functools.partial(kernel, cols, rows, layers, chunks),
        out_shape=jax.ShapeDtypeStruct((ns, blk, blk), jnp.bfloat16),
        in_specs=[pl.BlockSpec(memory_space=pltpu.HBM)] * 4,
        out_specs=pl.BlockSpec(memory_space=pltpu.VMEM),
        scratch_shapes=[
            pltpu.VMEM((ns, blk, blk), jnp.bfloat16),
            pltpu.SMEM(left_index.shape, jnp.int32),
            pltpu.SMEM(right_index.shape, jnp.int32),
            pltpu.SMEM(pair_count.shape, jnp.int32),
            pltpu.VMEM((cols,) + packed, jnp.bfloat16),
            pltpu.VMEM((group,) + packed, jnp.bfloat16),
            pltpu.VMEM((3 * half, blk, 2 * blk), jnp.bfloat16),
            pltpu.VMEM((ns + 1, blk, 2 * blk), jnp.bfloat16),
            pltpu.VMEM((ns, blk, 2 * blk), jnp.float32),
            pltpu.SemaphoreType.DMA,
            pltpu.SemaphoreType.DMA((3,)),
            pltpu.SemaphoreType.DMA((2, cols, chunks)),
            pltpu.SemaphoreType.DMA((cols, chunks)),
            pltpu.SemaphoreType.DMA((rows,)),
            pltpu.SemaphoreType.DMA((layers, rows)),
            pltpu.SemaphoreType.DMA((group,)),
        ],
        compiler_params=pltpu.CompilerParams(
            collective_id=0, has_side_effects=True, vmem_limit_bytes=60 * 1024 * 1024
        ),
    )(density_blocks, left_index, right_index, pair_count)


def solution(mesh):
    placed = (
        P(("parts", "layer", "row"), "col", None),
        P(("parts", "row"), "col", None),
        P(("parts", "row"), "col", None),
        P(("parts", "row"), "col"),
    )
    return jax.shard_map(
        on_device,
        mesh=mesh,
        in_specs=placed,
        out_specs=P(("parts", "layer", "row"), "col", None),
        check_vma=False,
    )
```

```python
import functools

import jax
import jax.numpy as jnp
from jax import lax
from jax.experimental import pallas as pl
from jax.experimental.pallas import tpu as pltpu
from jax.sharding import PartitionSpec as P

UNROLL = 24
MESH = pl.DeviceIdType.MESH


def kernel(
    cols, rows, layers, chunks,
    x_hbm, li_hbm, ri_hbm, cnt_hbm, out_ref,
    x_v, li_s, ri_s, cnt_s, lefts, rights, work_l, work_r, acc,
    in_sem, idx_sem, send_z, recv_z, send_x, send_l, recv_x,
):
    ns, blk, _ = x_hbm.shape
    half = ns // 2
    step_rows = half // chunks
    pairs = li_hbm.shape[1]
    c = lax.axis_index("col")
    layer = lax.axis_index("layer")
    row = lax.axis_index("row")
    r = layer * rows + row

    x_copy = pltpu.make_async_copy(x_hbm, x_v, in_sem)
    x_copy.start()
    idx_copies = [
        pltpu.make_async_copy(src, dst, idx_sem.at[j])
        for j, (src, dst) in enumerate(((li_hbm, li_s), (ri_hbm, ri_s), (cnt_hbm, cnt_s)))
    ]
    for copy in idx_copies:
        copy.start()

    barrier = pltpu.get_barrier_semaphore()

    @pl.when(c > 0)
    def _():
        pl.semaphore_signal(barrier, inc=1, device_id={"col": c - 1}, device_id_type=MESH)

    @pl.when(c < cols - 1)
    def _():
        pl.semaphore_signal(barrier, inc=1, device_id={"col": c + 1}, device_id_type=MESH)

    def row_mate(j):
        other = lax.rem(row + j, rows)
        return other, {"row": other}

    def layer_mate(j):
        other = lax.rem(layer + j, layers)
        return other, {"layer": other}

    for j in range(1, rows):
        pl.semaphore_signal(barrier, inc=1, device_id=row_mate(j)[1], device_id_type=MESH)
    for j in range(1, layers):
        pl.semaphore_signal(barrier, inc=1, device_id=layer_mate(j)[1], device_id_type=MESH)

    x_copy.wait()
    for s in range(half):
        both = jnp.concatenate([x_v[s], x_v[s + half]], axis=-1)
        lefts[c, s] = both
        rights[r, s] = both
    near = jnp.where(c > 0, 1, 0) + jnp.where(c < cols - 1, 1, 0)
    pl.semaphore_wait(barrier, near + (rows - 1) + (layers - 1))

    def z_copy(panel, chunk, way):
        part = lefts.at[panel, pl.ds(chunk * step_rows, step_rows)]
        return pltpu.make_async_remote_copy(
            src_ref=part,
            dst_ref=part,
            send_sem=send_z.at[way, panel, chunk],
            recv_sem=recv_z.at[panel, chunk],
            device_id={"col": c + (1 if way == 0 else -1)},
            device_id_type=MESH,
        )

    def row_copy(j):
        return pltpu.make_async_remote_copy(
            src_ref=lefts.at[c],
            dst_ref=rights.at[r],
            send_sem=send_x.at[j],
            recv_sem=recv_x.at[r],
            device_id=row_mate(j)[1],
            device_id_type=MESH,
        )

    def layer_copy(j, other):
        panel = layer * rows + other
        return pltpu.make_async_remote_copy(
            src_ref=rights.at[panel],
            dst_ref=rights.at[panel],
            send_sem=send_l.at[j, other],
            recv_sem=recv_x.at[panel],
            device_id=layer_mate(j)[1],
            device_id_type=MESH,
        )

    def right_landed(panel):
        pltpu.make_async_remote_copy(
            src_ref=rights.at[panel],
            dst_ref=rights.at[panel],
            send_sem=send_x.at[0],
            recv_sem=recv_x.at[panel],
            device_id=row_mate(1)[1],
            device_id_type=MESH,
        ).wait_recv()

    def on_way(way, do):
        pl.when(c < cols - 1 if way == 0 else c > 0)(do)

    for chunk in range(chunks):
        for way in (0, 1):
            on_way(way, lambda chunk=chunk, way=way: z_copy(c, chunk, way).start())
        if chunk == 0:
            for j in range(1, rows):
                row_copy(j).start()
            for j in range(1, layers):
                layer_copy(j, row).start()
    work_r[ns] = jnp.zeros_like(work_r[ns])
    acc[...] = jnp.zeros_like(acc)
    low = lax.broadcasted_iota(jnp.int32, (blk, 2 * blk), 1) < blk
    for copy in idx_copies:
        copy.wait()

    def multiply(k):
        @pl.when(k // rows != layer)
        def _():
            right_landed(k)

        for s in range(half):
            block = lefts[k, s]
            turned = jnp.concatenate([block[:, blk:], block[:, :blk]], axis=-1)
            work_l[s] = block
            work_l[s + half] = turned
            work_l[s + 2 * half] = block
            block = rights[k, s]
            work_r[s] = block
            work_r[s + half] = jnp.concatenate([block[:, blk:], block[:, :blk]], axis=-1)

        def one(o, carry):
            at = layer * ns + o
            count = cnt_s[k, at]
            left, right = [], []
            for p in range(0, pairs, 2):
                first = work_l[li_s[k, p, at]]
                second = work_l[li_s[k, p + 1, at] + half]
                left.append(jnp.where(low, first, second))
                for q in (p, p + 1):
                    right.append(work_r[jnp.where(q < count, ri_s[k, q, at], ns)])
            acc[o] += jnp.dot(
                jnp.concatenate(left, axis=1),
                jnp.concatenate(right, axis=0),
                preferred_element_type=jnp.float32,
            )
            return carry

        lax.fori_loop(0, ns, one, 0, unroll=UNROLL)

    shorter = jnp.minimum(c, cols - 1 - c)
    longer = jnp.maximum(c, cols - 1 - c)

    def turn(i):
        both = i <= 2 * shorter
        distance = jnp.where(both, (i + 1) // 2, i - shorter)
        lower = jnp.where(both, lax.rem(i, 2) == 1, c == longer)
        return jnp.where(lower, c - distance, c + distance)

    def landed(distance):
        return 1 + jnp.minimum(c, distance) + jnp.minimum(cols - 1 - c, distance)

    def multiply_turn(i, carry):
        multiply(turn(i))
        return carry

    def step(s, done):
        from_low = c - 1 - s
        from_high = c + 1 + s
        for chunk in range(chunks):

            @pl.when(from_low >= 0)
            def _(chunk=chunk):
                z_copy(from_low, chunk, 0).wait_recv()

                @pl.when(c < cols - 1)
                def _():
                    z_copy(from_low, chunk, 0).start()

            @pl.when(from_high < cols)
            def _(chunk=chunk):
                z_copy(from_high, chunk, 1).wait_recv()

                @pl.when(c > 0)
                def _():
                    z_copy(from_high, chunk, 1).start()

        @pl.when(s == 0)
        def _():
            for j in range(1, rows):
                other = row_mate(j)[0]
                right_landed(layer * rows + other)
                for to in range(1, layers):
                    layer_copy(to, other).start()

        eager = (shorter == 0) | (s + 1 >= longer)
        until = jnp.where(eager, landed(s + 1), landed(s))
        lax.fori_loop(done, until, multiply_turn, 0)
        return until

    lax.fori_loop(0, cols - 1, step, 0)

    for o in range(ns):
        out_ref[o] = acc[o][:, :blk].astype(out_ref.dtype)

    def drain(panel, carry):
        for chunk in range(chunks):

            @pl.when((c < cols - 1) & (panel <= c))
            def _(chunk=chunk):
                z_copy(panel, chunk, 0).wait_send()

            @pl.when((c > 0) & (panel >= c))
            def _(chunk=chunk):
                z_copy(panel, chunk, 1).wait_send()

        return carry

    lax.fori_loop(0, cols, drain, 0)
    for j in range(1, rows):
        row_copy(j).wait_send()
    for j in range(1, layers):
        for other in range(rows):
            layer_copy(j, other).wait_send()


def on_device(density_blocks, left_index, right_index, pair_count):
    ns, blk, _ = density_blocks.shape
    cols = lax.axis_size("col")
    rows = lax.axis_size("row")
    layers = lax.axis_size("layer")
    left_index = jnp.transpose(left_index, (1, 2, 0))
    right_index = jnp.transpose(right_index, (1, 2, 0))
    pair_count = jnp.transpose(pair_count, (1, 0))
    half = ns // 2
    chunks = 2 if half % 2 == 0 else 1
    group = rows * layers
    packed = (half, blk, 2 * blk)
    return pl.pallas_call(
        functools.partial(kernel, cols, rows, layers, chunks),
        out_shape=jax.ShapeDtypeStruct((ns, blk, blk), jnp.bfloat16),
        in_specs=[pl.BlockSpec(memory_space=pltpu.HBM)] * 4,
        out_specs=pl.BlockSpec(memory_space=pltpu.VMEM),
        scratch_shapes=[
            pltpu.VMEM((ns, blk, blk), jnp.bfloat16),
            pltpu.SMEM(left_index.shape, jnp.int32),
            pltpu.SMEM(right_index.shape, jnp.int32),
            pltpu.SMEM(pair_count.shape, jnp.int32),
            pltpu.VMEM((cols,) + packed, jnp.bfloat16),
            pltpu.VMEM((group,) + packed, jnp.bfloat16),
            pltpu.VMEM((3 * half, blk, 2 * blk), jnp.bfloat16),
            pltpu.VMEM((ns + 1, blk, 2 * blk), jnp.bfloat16),
            pltpu.VMEM((ns, blk, 2 * blk), jnp.float32),
            pltpu.SemaphoreType.DMA,
            pltpu.SemaphoreType.DMA((3,)),
            pltpu.SemaphoreType.DMA((2, cols, chunks)),
            pltpu.SemaphoreType.DMA((cols, chunks)),
            pltpu.SemaphoreType.DMA((rows,)),
            pltpu.SemaphoreType.DMA((layers, rows)),
            pltpu.SemaphoreType.DMA((group,)),
        ],
        compiler_params=pltpu.CompilerParams(
            collective_id=0, has_side_effects=True, vmem_limit_bytes=60 * 1024 * 1024
        ),
    )(density_blocks, left_index, right_index, pair_count)


def solution(mesh):
    placed = (
        P(("parts", "layer", "row"), "col", None),
        P(("parts", "row"), "col", None),
        P(("parts", "row"), "col", None),
        P(("parts", "row"), "col"),
    )
    return jax.shard_map(
        on_device,
        mesh=mesh,
        in_specs=placed,
        out_specs=P(("parts", "layer", "row"), "col", None),
        check_vma=False,
    )
```

```python
import functools

import jax
import jax.numpy as jnp
from jax import lax
from jax.experimental import pallas as pl
from jax.experimental.pallas import tpu as pltpu
from jax.sharding import PartitionSpec as P

UNROLL = 24
MESH = pl.DeviceIdType.MESH


def kernel(
    cols, rows, layers, chunks,
    x_hbm, li_hbm, ri_hbm, cnt_hbm, out_ref,
    x_v, li_s, ri_s, cnt_s, lefts, rights, work_l, work_r, acc,
    in_sem, idx_sem, send_z, recv_z, send_x, send_l, recv_x,
):
    ns, blk, _ = x_hbm.shape
    half = ns // 2
    step_rows = half // chunks
    pairs = li_hbm.shape[1]
    c = lax.axis_index("col")
    layer = lax.axis_index("layer")
    row = lax.axis_index("row")
    r = layer * rows + row

    def x_copy(chunk, side):
        part = pl.ds(side * half + chunk * step_rows, step_rows)
        return pltpu.make_async_copy(x_hbm.at[part], x_v.at[part], in_sem.at[chunk, side])

    for chunk in range(chunks):
        for side in (0, 1):
            x_copy(chunk, side).start()
    idx_copies = [
        pltpu.make_async_copy(src, dst, idx_sem.at[j])
        for j, (src, dst) in enumerate(((li_hbm, li_s), (ri_hbm, ri_s), (cnt_hbm, cnt_s)))
    ]
    for copy in idx_copies:
        copy.start()

    barrier = pltpu.get_barrier_semaphore()

    @pl.when(c > 0)
    def _():
        pl.semaphore_signal(barrier, inc=1, device_id={"col": c - 1}, device_id_type=MESH)

    @pl.when(c < cols - 1)
    def _():
        pl.semaphore_signal(barrier, inc=1, device_id={"col": c + 1}, device_id_type=MESH)

    def row_mate(j):
        other = lax.rem(row + j, rows)
        return other, {"row": other}

    def layer_mate(j):
        other = lax.rem(layer + j, layers)
        return other, {"layer": other}

    for j in range(1, rows):
        pl.semaphore_signal(barrier, inc=1, device_id=row_mate(j)[1], device_id_type=MESH)
    for j in range(1, layers):
        pl.semaphore_signal(barrier, inc=1, device_id=layer_mate(j)[1], device_id_type=MESH)

    near = jnp.where(c > 0, 1, 0) + jnp.where(c < cols - 1, 1, 0)
    pl.semaphore_wait(barrier, near + (rows - 1) + (layers - 1))

    def z_copy(panel, chunk, way):
        part = lefts.at[panel, pl.ds(chunk * step_rows, step_rows)]
        return pltpu.make_async_remote_copy(
            src_ref=part,
            dst_ref=part,
            send_sem=send_z.at[way, panel, chunk],
            recv_sem=recv_z.at[panel, chunk],
            device_id={"col": c + (1 if way == 0 else -1)},
            device_id_type=MESH,
        )

    def row_copy(j):
        return pltpu.make_async_remote_copy(
            src_ref=lefts.at[c],
            dst_ref=rights.at[r],
            send_sem=send_x.at[j],
            recv_sem=recv_x.at[r],
            device_id=row_mate(j)[1],
            device_id_type=MESH,
        )

    def layer_copy(j, other):
        panel = layer * rows + other
        return pltpu.make_async_remote_copy(
            src_ref=rights.at[panel],
            dst_ref=rights.at[panel],
            send_sem=send_l.at[j, other],
            recv_sem=recv_x.at[panel],
            device_id=layer_mate(j)[1],
            device_id_type=MESH,
        )

    def right_landed(panel):
        pltpu.make_async_remote_copy(
            src_ref=rights.at[panel],
            dst_ref=rights.at[panel],
            send_sem=send_x.at[0],
            recv_sem=recv_x.at[panel],
            device_id=row_mate(1)[1],
            device_id_type=MESH,
        ).wait_recv()

    def on_way(way, do):
        pl.when(c < cols - 1 if way == 0 else c > 0)(do)

    for chunk in range(chunks):
        for side in (0, 1):
            x_copy(chunk, side).wait()
        for t in range(chunk * step_rows, (chunk + 1) * step_rows):
            both = jnp.concatenate([x_v[t], x_v[t + half]], axis=-1)
            lefts[c, t] = both
            rights[r, t] = both
        for way in (0, 1):
            on_way(way, lambda chunk=chunk, way=way: z_copy(c, chunk, way).start())
    for j in range(1, rows):
        row_copy(j).start()
    for j in range(1, layers):
        layer_copy(j, row).start()
    work_r[ns] = jnp.zeros_like(work_r[ns])
    acc[...] = jnp.zeros_like(acc)
    low = lax.broadcasted_iota(jnp.int32, (blk, 2 * blk), 1) < blk
    for copy in idx_copies:
        copy.wait()

    def multiply(k):
        @pl.when(k // rows != layer)
        def _():
            right_landed(k)

        for s in range(half):
            block = lefts[k, s]
            turned = jnp.concatenate([block[:, blk:], block[:, :blk]], axis=-1)
            work_l[s] = block
            work_l[s + half] = turned
            work_l[s + 2 * half] = block
            block = rights[k, s]
            work_r[s] = block
            work_r[s + half] = jnp.concatenate([block[:, blk:], block[:, :blk]], axis=-1)

        def one(o, carry):
            at = layer * ns + o
            count = cnt_s[k, at]
            left, right = [], []
            for p in range(0, pairs, 2):
                first = work_l[li_s[k, p, at]]
                second = work_l[li_s[k, p + 1, at] + half]
                left.append(jnp.where(low, first, second))
                for q in (p, p + 1):
                    right.append(work_r[jnp.where(q < count, ri_s[k, q, at], ns)])
            acc[o] += jnp.dot(
                jnp.concatenate(left, axis=1),
                jnp.concatenate(right, axis=0),
                preferred_element_type=jnp.float32,
            )
            return carry

        lax.fori_loop(0, ns, one, 0, unroll=UNROLL)

    shorter = jnp.minimum(c, cols - 1 - c)
    longer = jnp.maximum(c, cols - 1 - c)

    def turn(i):
        both = i <= 2 * shorter
        distance = jnp.where(both, (i + 1) // 2, i - shorter)
        lower = jnp.where(both, lax.rem(i, 2) == 1, c == longer)
        return jnp.where(lower, c - distance, c + distance)

    def landed(distance):
        return 1 + jnp.minimum(c, distance) + jnp.minimum(cols - 1 - c, distance)

    def multiply_turn(i, carry):
        multiply(turn(i))
        return carry

    def step(s, done):
        from_low = c - 1 - s
        from_high = c + 1 + s
        for chunk in range(chunks):

            @pl.when(from_low >= 0)
            def _(chunk=chunk):
                z_copy(from_low, chunk, 0).wait_recv()

                @pl.when(c < cols - 1)
                def _():
                    z_copy(from_low, chunk, 0).start()

            @pl.when(from_high < cols)
            def _(chunk=chunk):
                z_copy(from_high, chunk, 1).wait_recv()

                @pl.when(c > 0)
                def _():
                    z_copy(from_high, chunk, 1).start()

        @pl.when(s == 0)
        def _():
            for j in range(1, rows):
                other = row_mate(j)[0]
                right_landed(layer * rows + other)
                for to in range(1, layers):
                    layer_copy(to, other).start()

        eager = (shorter == 0) | (s + 1 >= longer)
        until = jnp.where(eager, landed(s + 1), landed(s))
        lax.fori_loop(done, until, multiply_turn, 0)
        return until

    lax.fori_loop(0, cols - 1, step, 0)

    for o in range(ns):
        out_ref[o] = acc[o][:, :blk].astype(out_ref.dtype)

    def drain(panel, carry):
        for chunk in range(chunks):

            @pl.when((c < cols - 1) & (panel <= c))
            def _(chunk=chunk):
                z_copy(panel, chunk, 0).wait_send()

            @pl.when((c > 0) & (panel >= c))
            def _(chunk=chunk):
                z_copy(panel, chunk, 1).wait_send()

        return carry

    lax.fori_loop(0, cols, drain, 0)
    for j in range(1, rows):
        row_copy(j).wait_send()
    for j in range(1, layers):
        for other in range(rows):
            layer_copy(j, other).wait_send()


def on_device(density_blocks, left_index, right_index, pair_count):
    ns, blk, _ = density_blocks.shape
    cols = lax.axis_size("col")
    rows = lax.axis_size("row")
    layers = lax.axis_size("layer")
    left_index = jnp.transpose(left_index, (1, 2, 0))
    right_index = jnp.transpose(right_index, (1, 2, 0))
    pair_count = jnp.transpose(pair_count, (1, 0))
    half = ns // 2
    chunks = 2 if half % 2 == 0 else 1
    group = rows * layers
    packed = (half, blk, 2 * blk)
    return pl.pallas_call(
        functools.partial(kernel, cols, rows, layers, chunks),
        out_shape=jax.ShapeDtypeStruct((ns, blk, blk), jnp.bfloat16),
        in_specs=[pl.BlockSpec(memory_space=pltpu.HBM)] * 4,
        out_specs=pl.BlockSpec(memory_space=pltpu.VMEM),
        scratch_shapes=[
            pltpu.VMEM((ns, blk, blk), jnp.bfloat16),
            pltpu.SMEM(left_index.shape, jnp.int32),
            pltpu.SMEM(right_index.shape, jnp.int32),
            pltpu.SMEM(pair_count.shape, jnp.int32),
            pltpu.VMEM((cols,) + packed, jnp.bfloat16),
            pltpu.VMEM((group,) + packed, jnp.bfloat16),
            pltpu.VMEM((3 * half, blk, 2 * blk), jnp.bfloat16),
            pltpu.VMEM((ns + 1, blk, 2 * blk), jnp.bfloat16),
            pltpu.VMEM((ns, blk, 2 * blk), jnp.float32),
            pltpu.SemaphoreType.DMA((chunks, 2)),
            pltpu.SemaphoreType.DMA((3,)),
            pltpu.SemaphoreType.DMA((2, cols, chunks)),
            pltpu.SemaphoreType.DMA((cols, chunks)),
            pltpu.SemaphoreType.DMA((rows,)),
            pltpu.SemaphoreType.DMA((layers, rows)),
            pltpu.SemaphoreType.DMA((group,)),
        ],
        compiler_params=pltpu.CompilerParams(
            collective_id=0, has_side_effects=True, vmem_limit_bytes=60 * 1024 * 1024
        ),
    )(density_blocks, left_index, right_index, pair_count)


def solution(mesh):
    placed = (
        P(("parts", "layer", "row"), "col", None),
        P(("parts", "row"), "col", None),
        P(("parts", "row"), "col", None),
        P(("parts", "row"), "col"),
    )
    return jax.shard_map(
        on_device,
        mesh=mesh,
        in_specs=placed,
        out_specs=P(("parts", "layer", "row"), "col", None),
        check_vma=False,
    )
```
